512 devices in a mesh: dp: 16 (over z), work: 32 (over y, x, core).
Axes of the slice: x: 4, y: 4, z: 16, core: 2. Of those that a mesh axis runs over, the one named last changes fastest.
Arguments:
- grads: bfloat16 [16, 8192, 4096], P('dp', None, 'work')
- worker_list: int32 [16, 8, 2], P('dp'), may hold values from 0 to 3
Outputs:
- update: bfloat16 [8192, 4096], P('dp', 'work')
- worker_roots: bfloat16 [16, 32, 2, 512, 512], P('dp', 'work')
The draws below stay inside these ranges and needn't reach their ends.
Inputs may be any that keep to these rules, and one draw needn't show every extreme that they name: `worker_list`: each factor of each block has exactly one worker, among the four work devices that hold the block's columns.
All inputs are finite; a program needn't handle non-finite values.
Results may differ from the reference program's by a relative error of at most 0.039.
Values may be sent and summed in bfloat16 or wider, within the bound.
No kernel may reach another device: no remote copies, remote signals or barrier semaphores. Data moves between devices by JAX's collectives and lax.ppermute only.
A program may use at most 64 MiB of HBM per device.

```python
import jax
import jax.numpy as jnp
from jax import lax

BLOCK = 512
ITERS = 3
PIECE = 128
ROWS = 8192
COLS = 4096
QUADS = 8
N_DP = 16
N_WORK = 32


def draw_grads(key, part):
    key = jax.random.fold_in(key, 11)
    first, second, third = jax.random.split(key, 3)
    shape = (N_DP, ROWS, COLS)
    values = jax.random.normal(first, shape, jnp.float32)
    columns = jnp.arange(COLS)
    levels = (columns // PIECE % 4).astype(jnp.float32)
    factor = jnp.exp2(levels) * jnp.exp(jax.random.uniform(second, (COLS,), jnp.float32, -0.35, 0.35))
    order = jax.random.permutation(third, N_DP)
    row_block = jnp.arange(ROWS) // BLOCK
    heavy = 1.0 + 3.0 * (row_block[None, :] == order[:, None]).astype(jnp.float32)
    return (values * factor[None, None, :] * heavy[:, :, None] * (0.3 / jnp.sqrt(float(N_DP)))).astype(jnp.bfloat16)


def with_ends(drawn, key, least, largest):
    index_at = [jax.random.randint(jax.random.fold_in(key, axis), (), 0, length) for axis, length in enumerate(drawn.shape)]
    main_axis = drawn.shape.index(max(drawn.shape))
    beside = index_at[:main_axis] + [(index_at[main_axis] + 1) % drawn.shape[main_axis]] + index_at[main_axis + 1:]
    return drawn.at[tuple(index_at)].set(least).at[tuple(beside)].set(largest)


def setup_inputs(seed: int = 0) -> dict:
    key_list = jax.random.split(jax.random.key(seed), 3)
    return {
        "grads": draw_grads(jax.random.fold_in(key_list[2], 71), 0),
        "worker_list": with_ends(jax.random.randint(key_list[1], (N_DP, QUADS, 2), 0, 4), jax.random.fold_in(key_list[1], 1), 0, 3).astype(jnp.int32),
    }


def product(left, right):
    return jnp.dot(left.astype(jnp.float32), right.astype(jnp.float32), precision=lax.Precision.HIGHEST)

def inverse_root(stat):
    order = stat.shape[0]
    identity = jnp.eye(order, dtype=jnp.float32)
    damp = 0.1 * (jnp.trace(stat) / order + 1e-06)
    damped = stat + damp * identity
    scale = jnp.sqrt(jnp.sum(damped * damped) + 1e-06) * 0.25
    current = damped / scale
    iterate = identity
    for step in range(ITERS):
        factor = ((5.0 * identity - current) * 0.25).astype(jnp.bfloat16)
        square = product(factor, factor).astype(jnp.bfloat16)
        fourth = product(square, square).astype(jnp.bfloat16)
        current = product(fourth, current.astype(jnp.bfloat16))
        iterate = product(iterate.astype(jnp.bfloat16), factor)
    return (iterate * scale ** (-0.25)).astype(jnp.bfloat16)

def one_block(block):
    left_root = inverse_root(product(block, block.T))
    right_root = inverse_root(product(block.T, block))
    half = product(block, right_root).astype(jnp.bfloat16)
    raw = product(left_root, half)
    norm = jnp.sqrt(jnp.mean(raw * raw) + 1e-06)
    wide = block.astype(jnp.float32)
    graft = jnp.sqrt(jnp.mean(wide * wide) + 1e-06)
    return ((raw * (graft / norm)).astype(jnp.bfloat16), jnp.stack([left_root, right_root]))

def reference(grads, worker_list):
    summed = lax.optimization_barrier(jnp.sum(grads.astype(jnp.float32), axis=0)).astype(jnp.bfloat16)
    blocks = summed.reshape(N_DP, BLOCK, QUADS, BLOCK).transpose(0, 2, 1, 3).reshape(N_DP * QUADS, BLOCK, BLOCK)
    updates, roots = lax.map(one_block, blocks)
    update = updates.reshape(N_DP, QUADS, BLOCK, BLOCK).transpose(0, 2, 1, 3).reshape(ROWS, COLS)
    roots = roots.reshape(N_DP, QUADS, 2, BLOCK, BLOCK)
    picks = [jnp.where((worker_list == place)[:, :, :, None, None], roots, jnp.zeros((), jnp.bfloat16)) for place in range(4)]
    held = jnp.stack(picks, axis=2).reshape(N_DP, N_WORK, 2, BLOCK, BLOCK)
    return (update, held)
```

```python
import jax
import jax.numpy as jnp
from jax import lax
from jax.experimental import pallas as pl
from jax.experimental.pallas import tpu as pltpu
from jax.sharding import PartitionSpec as P

ITERS = 3
QUAD = 4


def product(left, right):
    return lax.dot_general(
        left, right, (((1,), (0,)), ((), ())), preferred_element_type=jnp.float32
    )


def gram_matrix(operand, contract):
    return lax.dot_general(
        operand, operand, (((contract,), (contract,)), ((), ())), preferred_element_type=jnp.float32
    )


def total(value):
    return jnp.sum(value, keepdims=True)


def newton_start(stat, diagonal):
    order = stat.shape[0]
    trace = total(jnp.where(diagonal, stat, 0.0))
    damp = 0.1 * (trace / order + 1e-06)
    damped = stat + jnp.where(diagonal, damp, 0.0)
    scale = jnp.sqrt(total(damped * damped) + 1e-06) * 0.25
    return damped * (1.0 / scale), scale


def newton_factor(current, diagonal):
    return ((jnp.where(diagonal, 5.0, 0.0) - current) * 0.25).astype(jnp.bfloat16)


def block_kernel(place_ref, block_ref, update_ref, held_ref, raw_ref):
    block = block_ref[...]
    order = block.shape[0]
    diagonal = lax.broadcasted_iota(jnp.int32, (order, order), 0) == lax.broadcasted_iota(
        jnp.int32, (order, order), 1
    )
    starts = [newton_start(gram_matrix(block, contract), diagonal) for contract in (1, 0)]
    currents = [start[0] for start in starts]
    iterates = [None, None]
    for step in range(ITERS):
        factors = [newton_factor(current, diagonal) for current in currents]
        if step < ITERS - 1:
            squares = [product(f, f).astype(jnp.bfloat16) for f in factors]
            fourths = [product(s, s).astype(jnp.bfloat16) for s in squares]
            currents = [
                product(fourth, current.astype(jnp.bfloat16))
                for fourth, current in zip(fourths, currents)
            ]
        if step == 0:
            iterates = factors
        else:
            iterates = [
                product(iterate.astype(jnp.bfloat16), factor)
                for iterate, factor in zip(iterates, factors)
            ]
    roots = [
        (iterate * lax.rsqrt(jnp.sqrt(start[1]))).astype(jnp.bfloat16)
        for iterate, start in zip(iterates, starts)
    ]
    for slot in range(2):
        held_ref[slot] = jnp.where(place_ref[1 + slot] != 0, roots[slot], jnp.zeros_like(roots[slot]))
    half = product(block, roots[1]).astype(jnp.bfloat16)
    raw = product(roots[0], half)
    raw_ref[...] = raw
    wide = block.astype(jnp.float32)
    count = order * order
    norm = jnp.sqrt(total(raw * raw) / count + 1e-06)
    graft = jnp.sqrt(total(wide * wide) / count + 1e-06)
    width = update_ref.shape[1]
    mine = raw_ref[:, pl.ds(pl.multiple_of(place_ref[0] * width, width), width)]
    update_ref[...] = (mine * (graft / norm)).astype(jnp.bfloat16)


def block_call(place, block, width):
    order = block.shape[0]
    return pl.pallas_call(
        block_kernel,
        out_shape=(
            jax.ShapeDtypeStruct((order, width), jnp.bfloat16),
            jax.ShapeDtypeStruct((2, order, order), jnp.bfloat16),
        ),
        in_specs=[
            pl.BlockSpec(memory_space=pltpu.SMEM),
            pl.BlockSpec(memory_space=pltpu.VMEM),
        ],
        out_specs=(
            pl.BlockSpec(memory_space=pltpu.VMEM),
            pl.BlockSpec(memory_space=pltpu.VMEM),
        ),
        scratch_shapes=[pltpu.VMEM((order, order), jnp.float32)],
        compiler_params=pltpu.CompilerParams(vmem_limit_bytes=48 * 1024 * 1024),
        cost_estimate=pl.CostEstimate(
            flops=40 * order**3, bytes_accessed=8 * order * order, transcendentals=0
        ),
        name="block_roots",
    )(place, block)


def local(grads, worker_list):
    index = lax.axis_index("work")
    place = index % QUAD
    assigned = lax.dynamic_index_in_dim(worker_list[0], index // QUAD, 0, keepdims=False)
    picks = jnp.concatenate([place[None], (assigned == place).astype(jnp.int32)])
    summed = lax.psum_scatter(grads[0], "dp", scatter_dimension=0, tiled=True)
    quads = lax.axis_size("work") // QUAD
    groups = [[QUAD * q + p for p in range(QUAD)] for q in range(quads)]
    block = lax.all_gather(summed, "work", axis=1, tiled=True, axis_index_groups=groups)
    update, held = block_call(picks, block, summed.shape[1])
    return (update, held[None, None])


def solution(mesh):
    placed = (P("dp", None, "work"), P("dp", None, None))
    return jax.shard_map(
        local,
        mesh=mesh,
        in_specs=placed,
        out_specs=(P("dp", "work"), P("dp", "work", None, None, None)),
        check_vma=False,
    )
```

```python
import functools

import jax
import jax.numpy as jnp
from jax import lax
from jax.experimental import pallas as pl
from jax.experimental.pallas import tpu as pltpu
from jax.sharding import PartitionSpec as P

ITERS = 3
QUAD = 4


def product(left, right):
    return lax.dot_general(
        left, right, (((1,), (0,)), ((), ())), preferred_element_type=jnp.float32
    )


def gram_matrix(operand, contract):
    return lax.dot_general(
        operand, operand, (((contract,), (contract,)), ((), ())), preferred_element_type=jnp.float32
    )


def total(value):
    return jnp.sum(value, keepdims=True)


def newton_start(stat, diagonal):
    order = stat.shape[0]
    trace = total(jnp.where(diagonal, stat, 0.0))
    damp = 0.1 * (trace / order + 1e-06)
    damped = stat + jnp.where(diagonal, damp, 0.0)
    scale = jnp.sqrt(total(damped * damped) + 1e-06) * 0.25
    return damped * (1.0 / scale), scale


def newton_factor(current, diagonal):
    return ((jnp.where(diagonal, 5.0, 0.0) - current) * 0.25).astype(jnp.bfloat16)


def block_kernel(place_ref, block_ref, update_ref, held_ref, raw_ref):
    block = block_ref[...]
    order = block.shape[0]
    diagonal = lax.broadcasted_iota(jnp.int32, (order, order), 0) == lax.broadcasted_iota(
        jnp.int32, (order, order), 1
    )
    starts = [newton_start(gram_matrix(block, contract), diagonal) for contract in (1, 0)]
    currents = [start[0] for start in starts]
    iterates = [None, None]
    for step in range(ITERS):
        factors = [newton_factor(current, diagonal) for current in currents]
        if step < ITERS - 1:
            squares = [product(f, f).astype(jnp.bfloat16) for f in factors]
            fourths = [product(s, s).astype(jnp.bfloat16) for s in squares]
            currents = [
                product(fourth, current.astype(jnp.bfloat16))
                for fourth, current in zip(fourths, currents)
            ]
        if step == 0:
            iterates = factors
        else:
            iterates = [
                product(iterate.astype(jnp.bfloat16), factor)
                for iterate, factor in zip(iterates, factors)
            ]
    roots = [
        (iterate * lax.rsqrt(jnp.sqrt(start[1]))).astype(jnp.bfloat16)
        for iterate, start in zip(iterates, starts)
    ]
    for slot in range(2):
        held_ref[slot] = jnp.where(place_ref[1 + slot] != 0, roots[slot], jnp.zeros_like(roots[slot]))
    half = product(block, roots[1]).astype(jnp.bfloat16)
    raw = product(roots[0], half)
    raw_ref[...] = raw
    wide = block.astype(jnp.float32)
    count = order * order
    norm = jnp.sqrt(total(raw * raw) / count + 1e-06)
    graft = jnp.sqrt(total(wide * wide) / count + 1e-06)
    width = update_ref.shape[1]
    mine = raw_ref[:, pl.ds(pl.multiple_of(place_ref[0] * width, width), width)]
    update_ref[...] = (mine * (graft / norm)).astype(jnp.bfloat16)


def block_call(place, block, width):
    order = block.shape[0]
    return pl.pallas_call(
        block_kernel,
        out_shape=(
            jax.ShapeDtypeStruct((order, width), jnp.bfloat16),
            jax.ShapeDtypeStruct((2, order, order), jnp.bfloat16),
        ),
        in_specs=[
            pl.BlockSpec(memory_space=pltpu.SMEM),
            pl.BlockSpec(memory_space=pltpu.VMEM),
        ],
        out_specs=(
            pl.BlockSpec(memory_space=pltpu.VMEM),
            pl.BlockSpec(memory_space=pltpu.VMEM),
        ),
        scratch_shapes=[pltpu.VMEM((order, order), jnp.float32)],
        compiler_params=pltpu.CompilerParams(vmem_limit_bytes=48 * 1024 * 1024),
        cost_estimate=pl.CostEstimate(
            flops=40 * order**3, bytes_accessed=8 * order * order, transcendentals=0
        ),
        name="block_roots",
    )(place, block)


def add_kernel(parts, parity_ref, *refs):
    *operands, out_ref = refs
    rows = out_ref.shape[0]
    summed = None
    for operand, (start, only) in zip(operands, parts):
        value = operand[pl.ds(start, rows), :].astype(jnp.float32)
        if only is not None:
            value = jnp.where(parity_ref[0] == only, value, 0.0)
        summed = value if summed is None else summed + value
    out_ref[...] = summed.astype(jnp.bfloat16)


def add_pieces(parity, rows, name, *terms):
    arrays = [term[0] for term in terms]
    width = arrays[0].shape[1]
    vmem = pl.BlockSpec(memory_space=pltpu.VMEM)
    return pl.pallas_call(
        functools.partial(add_kernel, [term[1:] for term in terms]),
        out_shape=jax.ShapeDtypeStruct((rows, width), jnp.bfloat16),
        in_specs=[pl.BlockSpec(memory_space=pltpu.SMEM)] + [vmem] * len(arrays),
        out_specs=vmem,
        compiler_params=pltpu.CompilerParams(vmem_limit_bytes=16 * 1024 * 1024),
        cost_estimate=pl.CostEstimate(
            flops=len(arrays) * rows * width,
            bytes_accessed=2 * (len(arrays) + 1) * rows * width,
            transcendentals=0,
        ),
        name=name,
    )(parity, *arrays)


def summed_piece(grads):
    size = lax.axis_size("dp")
    place = lax.axis_index("dp")
    pieces = grads.reshape(size, grads.shape[0] // size, grads.shape[1])
    rows = pieces.shape[1]
    own = {
        step: lax.dynamic_index_in_dim(pieces, (place + step) % size, 0, keepdims=False)
        for step in range(-8, 8)
    }
    parity = (place % 2)[None].astype(jnp.int32)

    def shifted(value, step):
        return lax.ppermute(value, "dp", [(i, (i + step) % size) for i in range(size)])

    def two(first, second):
        return jnp.concatenate([own[first], own[second]], 0)

    far = {side: shifted(two(7 * side, 5 * side), side) for side in (1, -1)}
    opposite = lax.ppermute(
        own[-8], "dp", [(i, (i + (2 if i % 2 == 0 else -2)) % size) for i in range(size)]
    )
    near = {side: shifted(two(3 * side, side), side) for side in (1, -1)}
    six, two_away, four = {}, {}, {}
    for side, only in ((1, 0), (-1, 1)):
        joined = add_pieces(
            parity, rows, "join_six", (far[side], 0, None), (own[6 * side], 0, None), (opposite, 0, only)
        )
        six[side] = shifted(joined, 2 * side)
    for side in (1, -1):
        joined = add_pieces(parity, rows, "join_two", (near[side], 0, None), (own[2 * side], 0, None))
        two_away[side] = shifted(joined, 2 * side)
    for side in (1, -1):
        joined = add_pieces(
            parity, rows, "join_four", (far[side], rows, None), (own[4 * side], 0, None), (six[side], 0, None)
        )
        four[side] = shifted(joined, 4 * side)
    return add_pieces(
        parity,
        rows,
        "join_all",
        (own[0], 0, None),
        (near[1], rows, None),
        (near[-1], rows, None),
        (two_away[1], 0, None),
        (two_away[-1], 0, None),
        (four[1], 0, None),
        (four[-1], 0, None),
    )


def local(grads, worker_list):
    index = lax.axis_index("work")
    place = index % QUAD
    assigned = lax.dynamic_index_in_dim(worker_list[0], index // QUAD, 0, keepdims=False)
    picks = jnp.concatenate([place[None], (assigned == place).astype(jnp.int32)])
    summed = summed_piece(grads[0])
    quads = lax.axis_size("work") // QUAD
    groups = [[QUAD * q + p for p in range(QUAD)] for q in range(quads)]
    block = lax.all_gather(summed, "work", axis=1, tiled=True, axis_index_groups=groups)
    update, held = block_call(picks, block, summed.shape[1])
    return (update, held[None, None])


def solution(mesh):
    placed = (P("dp", None, "work"), P("dp", None, None))
    return jax.shard_map(
        local,
        mesh=mesh,
        in_specs=placed,
        out_specs=(P("dp", "work"), P("dp", "work", None, None, None)),
        check_vma=False,
    )
```

```python
import functools

import jax
import jax.numpy as jnp
from jax import lax
from jax.experimental import pallas as pl
from jax.experimental.pallas import tpu as pltpu
from jax.sharding import PartitionSpec as P

QUAD = 4


def product(left, right, contract=((1,), (0,))):
    return lax.dot_general(left, right, (contract, ((), ())), preferred_element_type=jnp.float32)


def total(value):
    return jnp.sum(value, keepdims=True)


def symmetric_product(left, right):
    half = left.shape[0] // 2
    return (
        product(left[:half, :], right[...]),
        product(left[half:, :], right[:, half:]),
    )


def gram_matrix(block, contract):
    half = block.shape[0] // 2
    if contract == 1:
        first, second = block[:half, :], block[half:, :]
    else:
        first, second = block[:, :half], block[:, half:]
    dims = ((contract,), (contract,))
    return product(first, block[...], dims), product(second, second, dims)


def fill_symmetric(target, upper, corner):
    half = corner.shape[0]
    rounded = upper.astype(jnp.bfloat16)
    target[:half, :] = rounded
    target[half:, half:] = corner.astype(jnp.bfloat16)
    target[half:, :half] = rounded[:, half:].T


def fill_current_and_factor(current, factor, first, side, second, diagonal):
    half = first.shape[0]
    rounded = side.astype(jnp.bfloat16)
    turned = rounded.T
    quarter = jnp.bfloat16(-0.25)
    if current is not None:
        current[:half, :half] = first.astype(jnp.bfloat16)
        current[half:, half:] = second.astype(jnp.bfloat16)
        current[:half, half:] = rounded
        current[half:, :half] = turned
    ends = jnp.where(diagonal, 1.25, 0.0)
    factor[:half, :half] = (ends - first * 0.25).astype(jnp.bfloat16)
    factor[half:, half:] = (ends - second * 0.25).astype(jnp.bfloat16)
    factor[:half, half:] = rounded * quarter
    factor[half:, :half] = turned * quarter


def block_kernel(place_ref, block_ref, update_ref, held_ref, raw_ref, work_ref):
    order = block_ref.shape[0]
    half = order // 2
    both = (0, 1)
    current0, factor0, square, fourth, current1, factor1, iterate, factor2, root = range(9)

    def slot(side, name):
        return work_ref.at[side, name]

    block = block_ref[...].astype(jnp.float32)
    trace = total(block * block)
    damp = 0.1 * (trace / order + 1e-06)
    diagonal = lax.broadcasted_iota(jnp.int32, (half, half), 0) == lax.broadcasted_iota(
        jnp.int32, (half, half), 1
    )
    stats = [gram_matrix(block_ref, contract) for contract in (1, 0)]
    upper, corner = stats[0]
    first, side = upper[:, :half], upper[:, half:]
    squares = total(first * first) + 2.0 * total(side * side) + total(corner * corner)
    scale = jnp.sqrt(squares + damp * (2.0 * trace + order * damp) + 1e-06) * 0.25
    inverse = 1.0 / scale
    shift = jnp.where(diagonal, damp * inverse, 0.0)
    for k in both:
        upper, corner = stats[k]
        fill_current_and_factor(
            slot(k, current0),
            slot(k, factor0),
            upper[:, :half] * inverse + shift,
            upper[:, half:] * inverse,
            corner * inverse + shift,
            diagonal,
        )
    for now, factor, after, factor_after in (
        (current0, factor0, current1, factor1),
        (current1, factor1, None, factor2),
    ):
        for k in both:
            fill_symmetric(slot(k, square), *symmetric_product(slot(k, factor), slot(k, factor)))
        for k in both:
            fill_symmetric(slot(k, fourth), *symmetric_product(slot(k, square), slot(k, square)))
        if factor == factor1:
            for k in both:
                fill_symmetric(
                    slot(k, iterate), *symmetric_product(slot(k, factor0), slot(k, factor1))
                )
        for k in both:
            upper, corner = symmetric_product(slot(k, fourth), slot(k, now))
            fill_current_and_factor(
                None if after is None else slot(k, after),
                slot(k, factor_after),
                upper[:, :half],
                upper[:, half:],
                corner,
                diagonal,
            )
    power = lax.rsqrt(jnp.sqrt(scale))
    for k in (1, 0):
        upper, corner = symmetric_product(slot(k, iterate), slot(k, factor2))
        fill_symmetric(slot(k, root), upper * power, corner * power)
    for k in both:
        made = work_ref[k, root]
        held_ref[k] = jnp.where(place_ref[1 + k] != 0, made, jnp.zeros_like(made))
    half_done = product(block_ref[...], work_ref[1, root]).astype(jnp.bfloat16)
    raw = product(work_ref[0, root], half_done)
    raw_ref[...] = raw
    count = order * order
    norm = jnp.sqrt(total(raw * raw) / count + 1e-06)
    graft = jnp.sqrt(trace / count + 1e-06)
    width = update_ref.shape[1]
    mine = raw_ref[:, pl.ds(pl.multiple_of(place_ref[0] * width, width), width)]
    update_ref[...] = (mine * (graft / norm)).astype(jnp.bfloat16)


def block_call(place, block, width):
    order = block.shape[0]
    return pl.pallas_call(
        block_kernel,
        out_shape=(
            jax.ShapeDtypeStruct((order, width), jnp.bfloat16),
            jax.ShapeDtypeStruct((2, order, order), jnp.bfloat16),
        ),
        in_specs=[
            pl.BlockSpec(memory_space=pltpu.SMEM),
            pl.BlockSpec(memory_space=pltpu.VMEM),
        ],
        out_specs=(
            pl.BlockSpec(memory_space=pltpu.VMEM),
            pl.BlockSpec(memory_space=pltpu.VMEM),
        ),
        scratch_shapes=[
            pltpu.VMEM((order, order), jnp.float32),
            pltpu.VMEM((2, 9, order, order), jnp.bfloat16),
        ],
        compiler_params=pltpu.CompilerParams(vmem_limit_bytes=48 * 1024 * 1024),
        cost_estimate=pl.CostEstimate(
            flops=31 * order**3, bytes_accessed=8 * order * order, transcendentals=0
        ),
        name="block_roots",
    )(place, block)


def add_kernel(parts, parity_ref, *refs):
    *operands, out_ref = refs
    rows = out_ref.shape[0]
    summed = None
    for operand, (start, only) in zip(operands, parts):
        value = operand[pl.ds(start, rows), :].astype(jnp.float32)
        if only is not None:
            value = jnp.where(parity_ref[0] == only, value, 0.0)
        summed = value if summed is None else summed + value
    out_ref[...] = summed.astype(jnp.bfloat16)


def add_pieces(parity, rows, name, *terms):
    arrays = [term[0] for term in terms]
    width = arrays[0].shape[1]
    vmem = pl.BlockSpec(memory_space=pltpu.VMEM)
    return pl.pallas_call(
        functools.partial(add_kernel, [term[1:] for term in terms]),
        out_shape=jax.ShapeDtypeStruct((rows, width), jnp.bfloat16),
        in_specs=[pl.BlockSpec(memory_space=pltpu.SMEM)] + [vmem] * len(arrays),
        out_specs=vmem,
        compiler_params=pltpu.CompilerParams(vmem_limit_bytes=16 * 1024 * 1024),
        cost_estimate=pl.CostEstimate(
            flops=len(arrays) * rows * width,
            bytes_accessed=2 * (len(arrays) + 1) * rows * width,
            transcendentals=0,
        ),
        name=name,
    )(parity, *arrays)


def summed_piece(grads):
    size = lax.axis_size("dp")
    place = lax.axis_index("dp")
    pieces = grads.reshape(size, grads.shape[0] // size, grads.shape[1])
    rows = pieces.shape[1]
    own = {
        step: lax.dynamic_index_in_dim(pieces, (place + step) % size, 0, keepdims=False)
        for step in range(-8, 8)
    }
    parity = (place % 2)[None].astype(jnp.int32)

    def shifted(value, step):
        return lax.ppermute(value, "dp", [(i, (i + step) % size) for i in range(size)])

    def two(first, second):
        return jnp.concatenate([own[first], own[second]], 0)

    far = {side: shifted(two(7 * side, 5 * side), side) for side in (-1, 1)}
    opposite = lax.ppermute(
        own[-8], "dp", [(i, (i + (2 if i % 2 == 0 else -2)) % size) for i in range(size)]
    )
    near = {side: shifted(two(3 * side, side), side) for side in (-1, 1)}
    six, two_away, four = {}, {}, {}
    for side, only in ((-1, 1), (1, 0)):
        joined = add_pieces(
            parity, rows, "join_six", (far[side], 0, None), (own[6 * side], 0, None), (opposite, 0, only)
        )
        six[side] = shifted(joined, 2 * side)
    for side in (-1, 1):
        joined = add_pieces(parity, rows, "join_two", (near[side], 0, None), (own[2 * side], 0, None))
        two_away[side] = shifted(joined, 2 * side)
    for side in (-1, 1):
        joined = add_pieces(
            parity, rows, "join_four", (far[side], rows, None), (own[4 * side], 0, None), (six[side], 0, None)
        )
        four[side] = shifted(joined, 4 * side)
    return add_pieces(
        parity,
        rows,
        "join_all",
        (own[0], 0, None),
        (near[1], rows, None),
        (near[-1], rows, None),
        (two_away[1], 0, None),
        (two_away[-1], 0, None),
        (four[1], 0, None),
        (four[-1], 0, None),
    )


def local(grads, worker_list):
    index = lax.axis_index("work")
    place = index % QUAD
    assigned = lax.dynamic_index_in_dim(worker_list[0], index // QUAD, 0, keepdims=False)
    picks = jnp.concatenate([place[None], (assigned == place).astype(jnp.int32)])
    summed = summed_piece(grads[0])
    quads = lax.axis_size("work") // QUAD
    groups = [[QUAD * q + p for p in range(QUAD)] for q in range(quads)]
    block = lax.all_gather(summed, "work", axis=1, tiled=True, axis_index_groups=groups)
    update, held = block_call(picks, block, summed.shape[1])
    return (update, held[None, None])


def solution(mesh):
    placed = (P("dp", None, "work"), P("dp", None, None))
    return jax.shard_map(
        local,
        mesh=mesh,
        in_specs=placed,
        out_specs=(P("dp", "work"), P("dp", "work", None, None, None)),
        check_vma=False,
    )
```

```python
import functools

import jax
import jax.numpy as jnp
from jax import lax
from jax.experimental import pallas as pl
from jax.experimental.pallas import tpu as pltpu
from jax.sharding import PartitionSpec as P

QUAD = 4


def product(left, right, contract=((1,), (0,))):
    return lax.dot_general(left, right, (contract, ((), ())), preferred_element_type=jnp.float32)


def total(value):
    return jnp.sum(value, keepdims=True)


def symmetric_product(left, right):
    half = left.shape[0] // 2
    return (
        product(left[:half, :], right[...]),
        product(left[half:, :], right[:, half:]),
    )


def gram_matrix(block, contract):
    half = block.shape[0] // 2
    if contract == 1:
        first, second = block[:half, :], block[half:, :]
    else:
        first, second = block[:, :half], block[:, half:]
    dims = ((contract,), (contract,))
    return product(first, block[...], dims), product(second, second, dims)


def fill_symmetric(target, upper, corner):
    half = corner.shape[0]
    rounded = upper.astype(jnp.bfloat16)
    target[:half, :] = rounded
    target[half:, half:] = corner.astype(jnp.bfloat16)
    target[half:, :half] = rounded[:, half:].T


def fill_current_and_factor(current, factor, first, side, second, diagonal):
    half = first.shape[0]
    rounded = side.astype(jnp.bfloat16)
    turned = rounded.T
    quarter = jnp.bfloat16(-0.25)
    if current is not None:
        current[:half, :half] = first.astype(jnp.bfloat16)
        current[half:, half:] = second.astype(jnp.bfloat16)
        current[:half, half:] = rounded
        current[half:, :half] = turned
    ends = jnp.where(diagonal, 1.25, 0.0)
    factor[:half, :half] = (ends - first * 0.25).astype(jnp.bfloat16)
    factor[half:, half:] = (ends - second * 0.25).astype(jnp.bfloat16)
    factor[:half, half:] = rounded * quarter
    factor[half:, :half] = turned * quarter


def block_kernel(place_ref, block_ref, update_ref, held_ref, raw_ref, work_ref):
    order = block_ref.shape[0]
    half = order // 2
    both = (0, 1)
    current0, factor0, square, fourth, current1, factor1, iterate, factor2, root = range(9)

    def slot(side, name):
        return work_ref.at[side, name]

    block = block_ref[...].astype(jnp.float32)
    trace = total(block * block)
    damp = 0.1 * (trace / order + 1e-06)
    diagonal = lax.broadcasted_iota(jnp.int32, (half, half), 0) == lax.broadcasted_iota(
        jnp.int32, (half, half), 1
    )
    stats = [gram_matrix(block_ref, contract) for contract in (1, 0)]
    upper, corner = stats[0]
    first, side = upper[:, :half], upper[:, half:]
    squares = total(first * first) + 2.0 * total(side * side) + total(corner * corner)
    scale = jnp.sqrt(squares + damp * (2.0 * trace + order * damp) + 1e-06) * 0.25
    inverse = 1.0 / scale
    shift = jnp.where(diagonal, damp * inverse, 0.0)
    for k in both:
        upper, corner = stats[k]
        fill_current_and_factor(
            slot(k, current0),
            slot(k, factor0),
            upper[:, :half] * inverse + shift,
            upper[:, half:] * inverse,
            corner * inverse + shift,
            diagonal,
        )
    for now, factor, after, factor_after in (
        (current0, factor0, current1, factor1),
        (current1, factor1, None, factor2),
    ):
        for k in both:
            fill_symmetric(slot(k, square), *symmetric_product(slot(k, factor), slot(k, factor)))
        for k in both:
            fill_symmetric(slot(k, fourth), *symmetric_product(slot(k, square), slot(k, square)))
        if factor == factor1:
            for k in both:
                fill_symmetric(
                    slot(k, iterate), *symmetric_product(slot(k, factor0), slot(k, factor1))
                )
        for k in both:
            upper, corner = symmetric_product(slot(k, fourth), slot(k, now))
            fill_current_and_factor(
                None if after is None else slot(k, after),
                slot(k, factor_after),
                upper[:, :half],
                upper[:, half:],
                corner,
                diagonal,
            )
    power = lax.rsqrt(jnp.sqrt(scale))
    for k in (1, 0):
        upper, corner = symmetric_product(slot(k, iterate), slot(k, factor2))
        fill_symmetric(slot(k, root), upper * power, corner * power)
    for k in both:
        made = work_ref[k, root]
        held_ref[k] = jnp.where(place_ref[1 + k] != 0, made, jnp.zeros_like(made))
    half_done = product(block_ref[...], work_ref[1, root]).astype(jnp.bfloat16)
    raw = product(work_ref[0, root], half_done)
    raw_ref[...] = raw
    count = order * order
    norm = jnp.sqrt(total(raw * raw) / count + 1e-06)
    graft = jnp.sqrt(trace / count + 1e-06)
    width = update_ref.shape[1]
    mine = raw_ref[:, pl.ds(pl.multiple_of(place_ref[0] * width, width), width)]
    update_ref[...] = (mine * (graft / norm)).astype(jnp.bfloat16)


def block_call(place, block, width):
    order = block.shape[0]
    return pl.pallas_call(
        block_kernel,
        out_shape=(
            jax.ShapeDtypeStruct((order, width), jnp.bfloat16),
            jax.ShapeDtypeStruct((2, order, order), jnp.bfloat16),
        ),
        in_specs=[
            pl.BlockSpec(memory_space=pltpu.SMEM),
            pl.BlockSpec(memory_space=pltpu.VMEM),
        ],
        out_specs=(
            pl.BlockSpec(memory_space=pltpu.VMEM),
            pl.BlockSpec(memory_space=pltpu.VMEM),
        ),
        scratch_shapes=[
            pltpu.VMEM((order, order), jnp.float32),
            pltpu.VMEM((2, 9, order, order), jnp.bfloat16),
        ],
        compiler_params=pltpu.CompilerParams(vmem_limit_bytes=48 * 1024 * 1024),
        cost_estimate=pl.CostEstimate(
            flops=31 * order**3, bytes_accessed=8 * order * order, transcendentals=0
        ),
        name="block_roots",
    )(place, block)


def add_kernel(parts, parity_ref, *refs):
    *operands, out_ref = refs
    rows = out_ref.shape[0]
    summed = None
    for operand, (start, only) in zip(operands, parts):
        value = operand[pl.ds(start, rows), :].astype(jnp.float32)
        if only is not None:
            value = jnp.where(parity_ref[0] == only, value, 0.0)
        summed = value if summed is None else summed + value
    out_ref[...] = summed.astype(jnp.bfloat16)


def add_pieces(parity, rows, name, *terms):
    arrays = [term[0] for term in terms]
    width = arrays[0].shape[1]
    vmem = pl.BlockSpec(memory_space=pltpu.VMEM)
    return pl.pallas_call(
        functools.partial(add_kernel, [term[1:] for term in terms]),
        out_shape=jax.ShapeDtypeStruct((rows, width), jnp.bfloat16),
        in_specs=[pl.BlockSpec(memory_space=pltpu.SMEM)] + [vmem] * len(arrays),
        out_specs=vmem,
        compiler_params=pltpu.CompilerParams(vmem_limit_bytes=16 * 1024 * 1024),
        cost_estimate=pl.CostEstimate(
            flops=len(arrays) * rows * width,
            bytes_accessed=2 * (len(arrays) + 1) * rows * width,
            transcendentals=0,
        ),
        name=name,
    )(parity, *arrays)


def summed_piece(grads):
    size = lax.axis_size("dp")
    place = lax.axis_index("dp")
    pieces = grads.reshape(size, grads.shape[0] // size, grads.shape[1])
    rows = pieces.shape[1]
    own = {
        step: lax.dynamic_index_in_dim(pieces, (place + step) % size, 0, keepdims=False)
        for step in range(-8, 8)
    }
    parity = (place % 2)[None].astype(jnp.int32)

    def shifted(value, step):
        return lax.ppermute(value, "dp", [(i, (i + step) % size) for i in range(size)])

    def two(first, second):
        return jnp.concatenate([own[first], own[second]], 0)

    far = {side: shifted(two(7 * side, 5 * side), side) for side in (1, -1)}
    opposite = lax.ppermute(
        own[-8], "dp", [(i, (i + (2 if i % 2 == 0 else -2)) % size) for i in range(size)]
    )
    near = {side: shifted(two(3 * side, side), side) for side in (1, -1)}
    six, two_away, four = {}, {}, {}
    for side, only in ((1, 0), (-1, 1)):
        joined = add_pieces(
            parity, rows, "join_six", (far[side], 0, None), (own[6 * side], 0, None), (opposite, 0, only)
        )
        six[side] = shifted(joined, 2 * side)
    for side in (1, -1):
        joined = add_pieces(parity, rows, "join_two", (near[side], 0, None), (own[2 * side], 0, None))
        two_away[side] = shifted(joined, 2 * side)
    for side in (1, -1):
        joined = add_pieces(
            parity, rows, "join_four", (far[side], rows, None), (own[4 * side], 0, None), (six[side], 0, None)
        )
        four[side] = shifted(joined, 4 * side)
    return add_pieces(
        parity,
        rows,
        "join_all",
        (own[0], 0, None),
        (near[-1], rows, None),
        (near[1], rows, None),
        (two_away[1], 0, None),
        (two_away[-1], 0, None),
        (four[1], 0, None),
        (four[-1], 0, None),
    )


def local(grads, worker_list):
    index = lax.axis_index("work")
    place = index % QUAD
    assigned = lax.dynamic_index_in_dim(worker_list[0], index // QUAD, 0, keepdims=False)
    picks = jnp.concatenate([place[None], (assigned == place).astype(jnp.int32)])
    summed = summed_piece(grads[0])
    quads = lax.axis_size("work") // QUAD
    groups = [[QUAD * q + p for p in range(QUAD)] for q in range(quads)]
    block = lax.all_gather(summed, "work", axis=1, tiled=True, axis_index_groups=groups)
    update, held = block_call(picks, block, summed.shape[1])
    return (update, held[None, None])


def solution(mesh):
    placed = (P("dp", None, "work"), P("dp", None, None))
    return jax.shard_map(
        local,
        mesh=mesh,
        in_specs=placed,
        out_specs=(P("dp", "work"), P("dp", "work", None, None, None)),
        check_vma=False,
    )
```

```python
import functools

import jax
import jax.numpy as jnp
from jax import lax
from jax.experimental import pallas as pl
from jax.experimental.pallas import tpu as pltpu
from jax.sharding import PartitionSpec as P

QUAD = 4


def product(left, right, contract=((1,), (0,))):
    return lax.dot_general(left, right, (contract, ((), ())), preferred_element_type=jnp.float32)


def total(value):
    return jnp.sum(value, keepdims=True)


def symmetric_product(left, right):
    half = left.shape[0] // 2
    return (
        product(left[:half, :], right[...]),
        product(left[half:, :], right[:, half:]),
    )


def gram_matrix(block, contract):
    half = block.shape[0] // 2
    if contract == 1:
        first, second = block[:half, :], block[half:, :]
    else:
        first, second = block[:, :half], block[:, half:]
    dims = ((contract,), (contract,))
    return product(first, block[...], dims), product(second, second, dims)


def fill_symmetric(target, upper, corner):
    half = corner.shape[0]
    rounded = upper.astype(jnp.bfloat16)
    target[:half, :] = rounded
    target[half:, half:] = corner.astype(jnp.bfloat16)
    target[half:, :half] = rounded[:, half:].T


def fill_current_and_factor(current, factor, first, side, second, diagonal):
    half = first.shape[0]
    rounded = side.astype(jnp.bfloat16)
    turned = rounded.T
    quarter = jnp.bfloat16(-0.25)
    if current is not None:
        current[:half, :half] = first.astype(jnp.bfloat16)
        current[half:, half:] = second.astype(jnp.bfloat16)
        current[:half, half:] = rounded
        current[half:, :half] = turned
    ends = jnp.where(diagonal, 1.25, 0.0)
    factor[:half, :half] = (ends - first * 0.25).astype(jnp.bfloat16)
    factor[half:, half:] = (ends - second * 0.25).astype(jnp.bfloat16)
    factor[:half, half:] = rounded * quarter
    factor[half:, :half] = turned * quarter


def block_kernel(place_ref, block_ref, update_ref, held_ref, raw_ref, work_ref):
    order = block_ref.shape[0]
    half = order // 2
    both = (0, 1)
    current0, factor0, square, fourth, current1, factor1, iterate, factor2, root = range(9)

    def slot(side, name):
        return work_ref.at[side, name]

    block = block_ref[...].astype(jnp.float32)
    trace = total(block * block)
    damp = 0.1 * (trace / order + 1e-06)
    diagonal = lax.broadcasted_iota(jnp.int32, (half, half), 0) == lax.broadcasted_iota(
        jnp.int32, (half, half), 1
    )
    stats = [gram_matrix(block_ref, contract) for contract in (1, 0)]
    upper, corner = stats[0]
    first, side = upper[:, :half], upper[:, half:]
    squares = total(first * first) + 2.0 * total(side * side) + total(corner * corner)
    scale = jnp.sqrt(squares + damp * (2.0 * trace + order * damp) + 1e-06) * 0.25
    inverse = 1.0 / scale
    shift = jnp.where(diagonal, damp * inverse, 0.0)
    for k in both:
        upper, corner = stats[k]
        fill_current_and_factor(
            slot(k, current0),
            slot(k, factor0),
            upper[:, :half] * inverse + shift,
            upper[:, half:] * inverse,
            corner * inverse + shift,
            diagonal,
        )
    for now, factor, after, factor_after in (
        (current0, factor0, current1, factor1),
        (current1, factor1, None, factor2),
    ):
        for k in both:
            fill_symmetric(slot(k, square), *symmetric_product(slot(k, factor), slot(k, factor)))
        for k in both:
            fill_symmetric(slot(k, fourth), *symmetric_product(slot(k, square), slot(k, square)))
        if factor == factor1:
            for k in both:
                fill_symmetric(
                    slot(k, iterate), *symmetric_product(slot(k, factor0), slot(k, factor1))
                )
        for k in both:
            upper, corner = symmetric_product(slot(k, fourth), slot(k, now))
            fill_current_and_factor(
                None if after is None else slot(k, after),
                slot(k, factor_after),
                upper[:, :half],
                upper[:, half:],
                corner,
                diagonal,
            )
    power = lax.rsqrt(jnp.sqrt(scale))
    for k in (1, 0):
        upper, corner = symmetric_product(slot(k, iterate), slot(k, factor2))
        fill_symmetric(slot(k, root), upper * power, corner * power)
    for k in both:
        made = work_ref[k, root]
        held_ref[k] = jnp.where(place_ref[1 + k] != 0, made, jnp.zeros_like(made))
    half_done = product(block_ref[...], work_ref[1, root]).astype(jnp.bfloat16)
    raw = product(work_ref[0, root], half_done)
    raw_ref[...] = raw
    count = order * order
    norm = jnp.sqrt(total(raw * raw) / count + 1e-06)
    graft = jnp.sqrt(trace / count + 1e-06)
    width = update_ref.shape[1]
    mine = raw_ref[:, pl.ds(pl.multiple_of(place_ref[0] * width, width), width)]
    update_ref[...] = (mine * (graft / norm)).astype(jnp.bfloat16)


def block_call(place, block, width):
    order = block.shape[0]
    return pl.pallas_call(
        block_kernel,
        out_shape=(
            jax.ShapeDtypeStruct((order, width), jnp.bfloat16),
            jax.ShapeDtypeStruct((2, order, order), jnp.bfloat16),
        ),
        in_specs=[
            pl.BlockSpec(memory_space=pltpu.SMEM),
            pl.BlockSpec(memory_space=pltpu.VMEM),
        ],
        out_specs=(
            pl.BlockSpec(memory_space=pltpu.VMEM),
            pl.BlockSpec(memory_space=pltpu.VMEM),
        ),
        scratch_shapes=[
            pltpu.VMEM((order, order), jnp.float32),
            pltpu.VMEM((2, 9, order, order), jnp.bfloat16),
        ],
        compiler_params=pltpu.CompilerParams(vmem_limit_bytes=48 * 1024 * 1024),
        cost_estimate=pl.CostEstimate(
            flops=31 * order**3, bytes_accessed=8 * order * order, transcendentals=0
        ),
        name="block_roots",
    )(place, block)


OPPOSITE = "opposite"
ROUTE = (
    (1, (7, 5)),
    (-1, (-7, -5)),
    OPPOSITE,
    (-1, (-3, -1)),
    (1, (3, 1)),
    (2, (6,)),
    (-2, (-6,)),
    (-2, (-4,)),
    (2, (4,)),
    (2, (2,)),
    (-2, (-2,)),
)


def join_kernel(sums, parity_ref, *refs):
    *operands, out_ref = refs
    rows = out_ref.shape[0]
    summed = None
    for operand, start, only in sums:
        value = operands[operand][pl.ds(start, rows), :].astype(jnp.float32)
        if only is not None:
            value = jnp.where(parity_ref[0] == only, value, 0.0)
        summed = value if summed is None else summed + value
    out_ref[...] = summed.astype(jnp.bfloat16)


def join(parity, rows, name, terms):
    arrays = [term[0] for term in terms]
    width = arrays[0].shape[1]
    vmem = pl.BlockSpec(memory_space=pltpu.VMEM)
    return pl.pallas_call(
        functools.partial(join_kernel, [(k, *term[1:]) for k, term in enumerate(terms)]),
        out_shape=jax.ShapeDtypeStruct((rows, width), jnp.bfloat16),
        in_specs=[pl.BlockSpec(memory_space=pltpu.SMEM)] + [vmem] * len(arrays),
        out_specs=vmem,
        compiler_params=pltpu.CompilerParams(vmem_limit_bytes=16 * 1024 * 1024),
        cost_estimate=pl.CostEstimate(
            flops=len(arrays) * rows * width,
            bytes_accessed=2 * (len(arrays) + 1) * rows * width,
            transcendentals=0,
        ),
        name=name,
    )(parity, *arrays)


def summed_piece(grads):
    size = lax.axis_size("dp")
    place = lax.axis_index("dp")
    pieces = grads.reshape(size, grads.shape[0] // size, grads.shape[1])
    rows = pieces.shape[1]
    parity = (place % 2)[None].astype(jnp.int32)

    def own(distance):
        return lax.dynamic_index_in_dim(pieces, (place + distance) % size, 0, keepdims=False)

    def moved(value, shift):
        return lax.ppermute(value, "dp", [(i, (i + shift(i)) % size) for i in range(size)])

    terms = {distance: [(own(distance), 0, None)] for distance in range(-7, 8)}
    for step in ROUTE:
        if step == OPPOSITE:
            arrived = moved(own(-8), lambda i: 2 if i % 2 == 0 else -2)
            terms[6].append((arrived, 0, 0))
            terms[-6].append((arrived, 0, 1))
            continue
        shift, distances = step
        leaving = [terms.pop(distance) for distance in distances]
        if all(len(parts) == 1 for parts in leaving):
            value = jnp.concatenate([parts[0][0] for parts in leaving], 0)
        else:
            (parts,) = leaving
            value = join(parity, rows, "join_pieces", parts)
        arrived = moved(value, lambda i, shift=shift: shift)
        for order, distance in enumerate(distances):
            terms[distance - shift].append((arrived, order * rows, None))
    (parts,) = terms.values()
    return join(parity, rows, "join_all", parts)


def local(grads, worker_list):
    index = lax.axis_index("work")
    place = index % QUAD
    assigned = lax.dynamic_index_in_dim(worker_list[0], index // QUAD, 0, keepdims=False)
    picks = jnp.concatenate([place[None], (assigned == place).astype(jnp.int32)])
    summed = summed_piece(grads[0])
    quads = lax.axis_size("work") // QUAD
    groups = [[QUAD * q + p for p in range(QUAD)] for q in range(quads)]
    block = lax.all_gather(summed, "work", axis=1, tiled=True, axis_index_groups=groups)
    update, held = block_call(picks, block, summed.shape[1])
    return (update, held[None, None])


def solution(mesh):
    placed = (P("dp", None, "work"), P("dp", None, None))
    return jax.shard_map(
        local,
        mesh=mesh,
        in_specs=placed,
        out_specs=(P("dp", "work"), P("dp", "work", None, None, None)),
        check_vma=False,
    )
```

```python
import functools

import jax
import jax.numpy as jnp
from jax import lax
from jax.experimental import pallas as pl
from jax.experimental.pallas import tpu as pltpu
from jax.sharding import PartitionSpec as P

QUAD = 4


def product(left, right, contract=((1,), (0,))):
    return lax.dot_general(left, right, (contract, ((), ())), preferred_element_type=jnp.float32)


def total(value):
    return jnp.sum(value, keepdims=True)


def symmetric_product(left, right):
    half = left.shape[0] // 2
    return (
        product(left[:half, :], right[...]),
        product(left[half:, :], right[:, half:]),
    )


def gram_matrix(block, contract):
    half = block.shape[0] // 2
    if contract == 1:
        first, second = block[:half, :], block[half:, :]
    else:
        first, second = block[:, :half], block[:, half:]
    dims = ((contract,), (contract,))
    return product(first, block[...], dims), product(second, second, dims)


def fill_symmetric(target, upper, corner):
    half = corner.shape[0]
    rounded = upper.astype(jnp.bfloat16)
    target[:half, :] = rounded
    target[half:, half:] = corner.astype(jnp.bfloat16)
    target[half:, :half] = rounded[:, half:].T


def fill_current_and_factor(current, factor, first, side, second, diagonal):
    half = first.shape[0]
    rounded = side.astype(jnp.bfloat16)
    turned = rounded.T
    quarter = jnp.bfloat16(-0.25)
    if current is not None:
        current[:half, :half] = first.astype(jnp.bfloat16)
        current[half:, half:] = second.astype(jnp.bfloat16)
        current[:half, half:] = rounded
        current[half:, :half] = turned
    ends = jnp.where(diagonal, 1.25, 0.0)
    factor[:half, :half] = (ends - first * 0.25).astype(jnp.bfloat16)
    factor[half:, half:] = (ends - second * 0.25).astype(jnp.bfloat16)
    factor[:half, half:] = rounded * quarter
    factor[half:, :half] = turned * quarter


def block_kernel(place_ref, block_ref, update_ref, held_ref, raw_ref, work_ref):
    order = block_ref.shape[0]
    half = order // 2
    both = (0, 1)
    current0, factor0, square, fourth, current1, factor1, iterate, factor2, root = range(9)

    def slot(side, name):
        return work_ref.at[side, name]

    block = block_ref[...].astype(jnp.float32)
    trace = total(block * block)
    damp = 0.1 * (trace / order + 1e-06)
    diagonal = lax.broadcasted_iota(jnp.int32, (half, half), 0) == lax.broadcasted_iota(
        jnp.int32, (half, half), 1
    )
    stats = [gram_matrix(block_ref, contract) for contract in (1, 0)]
    upper, corner = stats[0]
    first, side = upper[:, :half], upper[:, half:]
    squares = total(first * first) + 2.0 * total(side * side) + total(corner * corner)
    scale = jnp.sqrt(squares + damp * (2.0 * trace + order * damp) + 1e-06) * 0.25
    inverse = 1.0 / scale
    shift = jnp.where(diagonal, damp * inverse, 0.0)
    for k in both:
        upper, corner = stats[k]
        fill_current_and_factor(
            slot(k, current0),
            slot(k, factor0),
            upper[:, :half] * inverse + shift,
            upper[:, half:] * inverse,
            corner * inverse + shift,
            diagonal,
        )
    for now, factor, after, factor_after in (
        (current0, factor0, current1, factor1),
        (current1, factor1, None, factor2),
    ):
        for k in both:
            fill_symmetric(slot(k, square), *symmetric_product(slot(k, factor), slot(k, factor)))
        for k in both:
            fill_symmetric(slot(k, fourth), *symmetric_product(slot(k, square), slot(k, square)))
        if factor == factor1:
            for k in both:
                fill_symmetric(
                    slot(k, iterate), *symmetric_product(slot(k, factor0), slot(k, factor1))
                )
        for k in both:
            upper, corner = symmetric_product(slot(k, fourth), slot(k, now))
            fill_current_and_factor(
                None if after is None else slot(k, after),
                slot(k, factor_after),
                upper[:, :half],
                upper[:, half:],
                corner,
                diagonal,
            )
    power = lax.rsqrt(jnp.sqrt(scale))
    for k in (1, 0):
        upper, corner = symmetric_product(slot(k, iterate), slot(k, factor2))
        fill_symmetric(slot(k, root), upper * power, corner * power)
    for k in both:
        made = work_ref[k, root]
        held_ref[k] = jnp.where(place_ref[1 + k] != 0, made, jnp.zeros_like(made))
    half_done = product(block_ref[...], work_ref[1, root]).astype(jnp.bfloat16)
    raw = product(work_ref[0, root], half_done)
    raw_ref[...] = raw
    count = order * order
    norm = jnp.sqrt(total(raw * raw) / count + 1e-06)
    graft = jnp.sqrt(trace / count + 1e-06)
    width = update_ref.shape[1]
    mine = raw_ref[:, pl.ds(pl.multiple_of(place_ref[0] * width, width), width)]
    update_ref[...] = (mine * (graft / norm)).astype(jnp.bfloat16)


def block_call(place, block, width):
    order = block.shape[0]
    return pl.pallas_call(
        block_kernel,
        out_shape=(
            jax.ShapeDtypeStruct((order, width), jnp.bfloat16),
            jax.ShapeDtypeStruct((2, order, order), jnp.bfloat16),
        ),
        in_specs=[
            pl.BlockSpec(memory_space=pltpu.SMEM),
            pl.BlockSpec(memory_space=pltpu.VMEM),
        ],
        out_specs=(
            pl.BlockSpec(memory_space=pltpu.VMEM),
            pl.BlockSpec(memory_space=pltpu.VMEM),
        ),
        scratch_shapes=[
            pltpu.VMEM((order, order), jnp.float32),
            pltpu.VMEM((2, 9, order, order), jnp.bfloat16),
        ],
        compiler_params=pltpu.CompilerParams(vmem_limit_bytes=48 * 1024 * 1024),
        cost_estimate=pl.CostEstimate(
            flops=31 * order**3, bytes_accessed=8 * order * order, transcendentals=0
        ),
        name="block_roots",
    )(place, block)


OPPOSITE = "opposite"
ROUTE = (
    (1, (7, 5)),
    (-1, (-7, -5)),
    OPPOSITE,
    (-1, (-3, -1)),
    (1, (3, 1)),
    (2, (6,)),
    (-2, (-6,)),
    (-2, (-2,)),
    (2, (2,)),
    (4, (4,)),
    (-4, (-4,)),
)


def join_kernel(sums, parity_ref, *refs):
    *operands, out_ref = refs
    rows = out_ref.shape[0]
    summed = None
    for operand, start, only in sums:
        value = operands[operand][pl.ds(start, rows), :].astype(jnp.float32)
        if only is not None:
            value = jnp.where(parity_ref[0] == only, value, 0.0)
        summed = value if summed is None else summed + value
    out_ref[...] = summed.astype(jnp.bfloat16)


def join(parity, rows, name, terms):
    arrays = [term[0] for term in terms]
    width = arrays[0].shape[1]
    vmem = pl.BlockSpec(memory_space=pltpu.VMEM)
    return pl.pallas_call(
        functools.partial(join_kernel, [(k, *term[1:]) for k, term in enumerate(terms)]),
        out_shape=jax.ShapeDtypeStruct((rows, width), jnp.bfloat16),
        in_specs=[pl.BlockSpec(memory_space=pltpu.SMEM)] + [vmem] * len(arrays),
        out_specs=vmem,
        compiler_params=pltpu.CompilerParams(vmem_limit_bytes=16 * 1024 * 1024),
        cost_estimate=pl.CostEstimate(
            flops=len(arrays) * rows * width,
            bytes_accessed=2 * (len(arrays) + 1) * rows * width,
            transcendentals=0,
        ),
        name=name,
    )(parity, *arrays)


def summed_piece(grads):
    size = lax.axis_size("dp")
    columns = lax.axis_size("work")
    place = lax.axis_index("dp")
    side = 1 - 2 * (lax.axis_index("work") % 2)
    pieces = grads.reshape(size, grads.shape[0] // size, grads.shape[1])
    rows = pieces.shape[1]
    parity = (place % 2)[None].astype(jnp.int32)

    def own(distance):
        return lax.dynamic_index_in_dim(pieces, (place + side * distance) % size, 0, keepdims=False)

    def moved(value, shift):
        pairs = [
            (i * columns + w, (i + (1 - 2 * (w % 2)) * shift(i)) % size * columns + w)
            for i in range(size)
            for w in range(columns)
        ]
        return lax.ppermute(value, ("dp", "work"), pairs)

    terms = {distance: [(own(distance), 0, None)] for distance in range(-7, 8)}
    for step in ROUTE:
        if step == OPPOSITE:
            arrived = moved(own(-8), lambda i: 2 if i % 2 == 0 else -2)
            terms[6].append((arrived, 0, 0))
            terms[-6].append((arrived, 0, 1))
            continue
        shift, distances = step
        leaving = [terms.pop(distance) for distance in distances]
        if all(len(parts) == 1 for parts in leaving):
            value = jnp.concatenate([parts[0][0] for parts in leaving], 0)
        else:
            (parts,) = leaving
            value = join(parity, rows, "join_pieces", parts)
        arrived = moved(value, lambda i, shift=shift: shift)
        for order, distance in enumerate(distances):
            terms[distance - shift].append((arrived, order * rows, None))
    (parts,) = terms.values()
    return join(parity, rows, "join_all", parts)


def local(grads, worker_list):
    index = lax.axis_index("work")
    place = index % QUAD
    assigned = lax.dynamic_index_in_dim(worker_list[0], index // QUAD, 0, keepdims=False)
    picks = jnp.concatenate([place[None], (assigned == place).astype(jnp.int32)])
    summed = summed_piece(grads[0])
    quads = lax.axis_size("work") // QUAD
    groups = [[QUAD * q + p for p in range(QUAD)] for q in range(quads)]
    block = lax.all_gather(summed, "work", axis=1, tiled=True, axis_index_groups=groups)
    update, held = block_call(picks, block, summed.shape[1])
    return (update, held[None, None])


def solution(mesh):
    placed = (P("dp", None, "work"), P("dp", None, None))
    return jax.shard_map(
        local,
        mesh=mesh,
        in_specs=placed,
        out_specs=(P("dp", "work"), P("dp", "work", None, None, None)),
        check_vma=False,
    )
```

```python
import functools

import jax
import jax.numpy as jnp
from jax import lax
from jax.experimental import pallas as pl
from jax.experimental.pallas import tpu as pltpu
from jax.sharding import PartitionSpec as P

QUAD = 4


def product(left, right, contract=((1,), (0,))):
    return lax.dot_general(left, right, (contract, ((), ())), preferred_element_type=jnp.float32)


def total(value):
    return jnp.sum(value, keepdims=True)


def symmetric_product(left, right):
    half = left.shape[0] // 2
    return (
        product(left[:half, :], right[...]),
        product(left[half:, :], right[:, half:]),
    )


def gram_matrix(block, contract):
    half = block.shape[0] // 2
    if contract == 1:
        first, second = block[:half, :], block[half:, :]
    else:
        first, second = block[:, :half], block[:, half:]
    dims = ((contract,), (contract,))
    return product(first, block[...], dims), product(second, second, dims)


def fill_symmetric(target, upper, corner):
    half = corner.shape[0]
    rounded = upper.astype(jnp.bfloat16)
    target[:half, :] = rounded
    target[half:, half:] = corner.astype(jnp.bfloat16)
    target[half:, :half] = rounded[:, half:].T


def fill_current_and_factor(current, factor, first, side, second, diagonal):
    half = first.shape[0]
    rounded = side.astype(jnp.bfloat16)
    turned = rounded.T
    quarter = jnp.bfloat16(-0.25)
    if current is not None:
        current[:half, :half] = first.astype(jnp.bfloat16)
        current[half:, half:] = second.astype(jnp.bfloat16)
        current[:half, half:] = rounded
        current[half:, :half] = turned
    ends = jnp.where(diagonal, 1.25, 0.0)
    factor[:half, :half] = (ends - first * 0.25).astype(jnp.bfloat16)
    factor[half:, half:] = (ends - second * 0.25).astype(jnp.bfloat16)
    factor[:half, half:] = rounded * quarter
    factor[half:, :half] = turned * quarter


def block_kernel(place_ref, block_ref, update_ref, held_ref, raw_ref, work_ref):
    order = block_ref.shape[0]
    half = order // 2
    both = (0, 1)
    current0, factor0, square, fourth, current1, factor1, iterate, factor2, root = range(9)

    def slot(side, name):
        return work_ref.at[side, name]

    block = block_ref[...].astype(jnp.float32)
    trace = total(block * block)
    damp = 0.1 * (trace / order + 1e-06)
    diagonal = lax.broadcasted_iota(jnp.int32, (half, half), 0) == lax.broadcasted_iota(
        jnp.int32, (half, half), 1
    )
    stats = [gram_matrix(block_ref, contract) for contract in (1, 0)]
    upper, corner = stats[0]
    first, side = upper[:, :half], upper[:, half:]
    squares = total(first * first) + 2.0 * total(side * side) + total(corner * corner)
    scale = jnp.sqrt(squares + damp * (2.0 * trace + order * damp) + 1e-06) * 0.25
    inverse = 1.0 / scale
    shift = jnp.where(diagonal, damp * inverse, 0.0)
    for k in both:
        upper, corner = stats[k]
        fill_current_and_factor(
            slot(k, current0),
            slot(k, factor0),
            upper[:, :half] * inverse + shift,
            upper[:, half:] * inverse,
            corner * inverse + shift,
            diagonal,
        )
    for now, factor, after, factor_after in (
        (current0, factor0, current1, factor1),
        (current1, factor1, None, factor2),
    ):
        for k in both:
            fill_symmetric(slot(k, square), *symmetric_product(slot(k, factor), slot(k, factor)))
        for k in both:
            fill_symmetric(slot(k, fourth), *symmetric_product(slot(k, square), slot(k, square)))
        if factor == factor1:
            for k in both:
                fill_symmetric(
                    slot(k, iterate), *symmetric_product(slot(k, factor0), slot(k, factor1))
                )
        for k in both:
            upper, corner = symmetric_product(slot(k, fourth), slot(k, now))
            fill_current_and_factor(
                None if after is None else slot(k, after),
                slot(k, factor_after),
                upper[:, :half],
                upper[:, half:],
                corner,
                diagonal,
            )
    power = lax.rsqrt(jnp.sqrt(scale))
    for k in (1, 0):
        upper, corner = symmetric_product(slot(k, iterate), slot(k, factor2))
        fill_symmetric(slot(k, root), upper * power, corner * power)
    for k in both:
        made = work_ref[k, root]
        held_ref[k] = jnp.where(place_ref[1 + k] != 0, made, jnp.zeros_like(made))
    half_done = product(block_ref[...], work_ref[1, root]).astype(jnp.bfloat16)
    raw = product(work_ref[0, root], half_done)
    raw_ref[...] = raw
    count = order * order
    norm = jnp.sqrt(total(raw * raw) / count + 1e-06)
    graft = jnp.sqrt(trace / count + 1e-06)
    width = update_ref.shape[1]
    mine = raw_ref[:, pl.ds(pl.multiple_of(place_ref[0] * width, width), width)]
    update_ref[...] = (mine * (graft / norm)).astype(jnp.bfloat16)


def block_call(place, block, width):
    order = block.shape[0]
    return pl.pallas_call(
        block_kernel,
        out_shape=(
            jax.ShapeDtypeStruct((order, width), jnp.bfloat16),
            jax.ShapeDtypeStruct((2, order, order), jnp.bfloat16),
        ),
        in_specs=[
            pl.BlockSpec(memory_space=pltpu.SMEM),
            pl.BlockSpec(memory_space=pltpu.VMEM),
        ],
        out_specs=(
            pl.BlockSpec(memory_space=pltpu.VMEM),
            pl.BlockSpec(memory_space=pltpu.VMEM),
        ),
        scratch_shapes=[
            pltpu.VMEM((order, order), jnp.float32),
            pltpu.VMEM((2, 9, order, order), jnp.bfloat16),
        ],
        compiler_params=pltpu.CompilerParams(vmem_limit_bytes=48 * 1024 * 1024),
        cost_estimate=pl.CostEstimate(
            flops=31 * order**3, bytes_accessed=8 * order * order, transcendentals=0
        ),
        name="block_roots",
    )(place, block)


OPPOSITE = "opposite"
ROUTE = (
    (1, (7, 5)),
    (-1, (-7, -5)),
    OPPOSITE,
    (-1, (-3, -1)),
    (1, (3, 1)),
    (2, (6,)),
    (-2, (-6,)),
    (-2, (-2,)),
    (2, (2,)),
    (4, (4,)),
    (-4, (-4,)),
)


def join_kernel(sums, parity_ref, *refs):
    *operands, out_ref = refs
    rows = out_ref.shape[0]
    summed = None
    for operand, start, only in sums:
        value = operands[operand][pl.ds(start, rows), :].astype(jnp.float32)
        if only is not None:
            value = jnp.where(parity_ref[0] == only, value, 0.0)
        summed = value if summed is None else summed + value
    out_ref[...] = summed.astype(jnp.bfloat16)


def join(parity, rows, name, terms):
    arrays = [term[0] for term in terms]
    width = arrays[0].shape[1]
    vmem = pl.BlockSpec(memory_space=pltpu.VMEM)
    return pl.pallas_call(
        functools.partial(join_kernel, [(k, *term[1:]) for k, term in enumerate(terms)]),
        out_shape=jax.ShapeDtypeStruct((rows, width), jnp.bfloat16),
        in_specs=[pl.BlockSpec(memory_space=pltpu.SMEM)] + [vmem] * len(arrays),
        out_specs=vmem,
        compiler_params=pltpu.CompilerParams(vmem_limit_bytes=16 * 1024 * 1024),
        cost_estimate=pl.CostEstimate(
            flops=len(arrays) * rows * width,
            bytes_accessed=2 * (len(arrays) + 1) * rows * width,
            transcendentals=0,
        ),
        name=name,
    )(parity, *arrays)


def fetch_kernel(groups, size, where_ref, pieces_ref, *refs):
    *out_refs, done = refs
    rows = pieces_ref.shape[1]
    copies = []
    for out_ref, distances in zip(out_refs, groups):
        for order, distance in enumerate(distances):
            index = lax.rem(where_ref[0] + where_ref[1] * distance + size, size)
            copies.append(
                pltpu.make_async_copy(
                    pieces_ref.at[index],
                    out_ref.at[pl.ds(order * rows, rows), :],
                    done.at[len(copies)],
                )
            )
    for copy in copies:
        copy.start()
    for copy in copies:
        copy.wait()


def fetch(where, pieces, groups):
    size, rows, width = pieces.shape
    return pl.pallas_call(
        functools.partial(fetch_kernel, groups, size),
        out_shape=[jax.ShapeDtypeStruct((len(g) * rows, width), pieces.dtype) for g in groups],
        in_specs=[pl.BlockSpec(memory_space=pltpu.SMEM), pl.BlockSpec(memory_space=pl.ANY)],
        out_specs=[pl.BlockSpec(memory_space=pltpu.VMEM)] * len(groups),
        scratch_shapes=[pltpu.SemaphoreType.DMA((sum(len(g) for g in groups),))],
        compiler_params=pltpu.CompilerParams(vmem_limit_bytes=50 * 1024 * 1024),
        cost_estimate=pl.CostEstimate(
            flops=0, bytes_accessed=4 * size * rows * width, transcendentals=0
        ),
        name="fetch_pieces",
    )(where, pieces)


def summed_piece(grads):
    size = lax.axis_size("dp")
    columns = lax.axis_size("work")
    place = lax.axis_index("dp")
    side = 1 - 2 * (lax.axis_index("work") % 2)
    pieces = grads.reshape(size, grads.shape[0] // size, grads.shape[1])
    rows = pieces.shape[1]
    parity = (place % 2)[None].astype(jnp.int32)

    def moved(value, shift):
        pairs = [
            (i * columns + w, (i + (1 - 2 * (w % 2)) * shift(i)) % size * columns + w)
            for i in range(size)
            for w in range(columns)
        ]
        return lax.ppermute(value, ("dp", "work"), pairs)

    messages, joined = [(-8,)], {6, -6}
    for step in ROUTE:
        if step != OPPOSITE:
            shift, distances = step
            if not joined.intersection(distances):
                messages.append(distances)
            joined.update(distance - shift for distance in distances)
    kept = [(distance,) for distance in range(-7, 8) if distance in joined]
    where = jnp.stack([place, side]).astype(jnp.int32)
    fetched = dict(zip(messages + kept, fetch(where, pieces, messages + kept)))

    terms = {distance: [(fetched[(distance,)], 0, None)] for (distance,) in kept}
    for step in ROUTE:
        if step == OPPOSITE:
            arrived = moved(fetched[(-8,)], lambda i: 2 if i % 2 == 0 else -2)
            terms[6].append((arrived, 0, 0))
            terms[-6].append((arrived, 0, 1))
            continue
        shift, distances = step
        if distances in messages:
            value = fetched[distances]
        else:
            (distance,) = distances
            value = join(parity, rows, "join_pieces", terms.pop(distance))
        arrived = moved(value, lambda i, shift=shift: shift)
        for order, distance in enumerate(distances):
            terms[distance - shift].append((arrived, order * rows, None))
    (parts,) = terms.values()
    return join(parity, rows, "join_all", parts)


def local(grads, worker_list):
    index = lax.axis_index("work")
    place = index % QUAD
    assigned = lax.dynamic_index_in_dim(worker_list[0], index // QUAD, 0, keepdims=False)
    picks = jnp.concatenate([place[None], (assigned == place).astype(jnp.int32)])
    summed = summed_piece(grads[0])
    quads = lax.axis_size("work") // QUAD
    groups = [[QUAD * q + p for p in range(QUAD)] for q in range(quads)]
    block = lax.all_gather(summed, "work", axis=1, tiled=True, axis_index_groups=groups)
    update, held = block_call(picks, block, summed.shape[1])
    return (update, held[None, None])


def solution(mesh):
    placed = (P("dp", None, "work"), P("dp", None, None))
    return jax.shard_map(
        local,
        mesh=mesh,
        in_specs=placed,
        out_specs=(P("dp", "work"), P("dp", "work", None, None, None)),
        check_vma=False,
    )
```

```python
import functools

import jax
import jax.numpy as jnp
from jax import lax
from jax.experimental import pallas as pl
from jax.experimental.pallas import tpu as pltpu
from jax.sharding import PartitionSpec as P

QUAD = 4


def product(left, right, contract=((1,), (0,))):
    return lax.dot_general(left, right, (contract, ((), ())), preferred_element_type=jnp.float32)


def total(value):
    return jnp.sum(value, keepdims=True)


def symmetric_product(left, right):
    half = left.shape[0] // 2
    return (
        product(left[:half, :], right[...]),
        product(left[half:, :], right[:, half:]),
    )


def gram_matrix(block, contract):
    half = block.shape[0] // 2
    if contract == 1:
        first, second = block[:half, :], block[half:, :]
    else:
        first, second = block[:, :half], block[:, half:]
    dims = ((contract,), (contract,))
    return product(first, block[...], dims), product(second, second, dims)


def fill_symmetric(target, upper, corner):
    half = corner.shape[0]
    rounded = upper.astype(jnp.bfloat16)
    target[:half, :] = rounded
    target[half:, half:] = corner.astype(jnp.bfloat16)
    target[half:, :half] = rounded[:, half:].T


def fill_current_and_factor(current, factor, first, side, second, diagonal):
    half = first.shape[0]
    rounded = side.astype(jnp.bfloat16)
    turned = rounded.T
    quarter = jnp.bfloat16(-0.25)
    if current is not None:
        current[:half, :half] = first.astype(jnp.bfloat16)
        current[half:, half:] = second.astype(jnp.bfloat16)
        current[:half, half:] = rounded
        current[half:, :half] = turned
    ends = jnp.where(diagonal, 1.25, 0.0)
    factor[:half, :half] = (ends - first * 0.25).astype(jnp.bfloat16)
    factor[half:, half:] = (ends - second * 0.25).astype(jnp.bfloat16)
    factor[:half, half:] = rounded * quarter
    factor[half:, :half] = turned * quarter


def block_kernel(place_ref, block_ref, update_ref, held_ref, raw_ref, work_ref):
    order = block_ref.shape[0]
    half = order // 2
    both = (0, 1)
    current0, factor0, square, fourth, current1, factor1, iterate, factor2, root = range(9)

    def slot(side, name):
        return work_ref.at[side, name]

    block = block_ref[...].astype(jnp.float32)
    trace = total(block * block)
    damp = 0.1 * (trace / order + 1e-06)
    diagonal = lax.broadcasted_iota(jnp.int32, (half, half), 0) == lax.broadcasted_iota(
        jnp.int32, (half, half), 1
    )
    stats = [gram_matrix(block_ref, contract) for contract in (1, 0)]
    upper, corner = stats[0]
    first, side = upper[:, :half], upper[:, half:]
    squares = total(first * first) + 2.0 * total(side * side) + total(corner * corner)
    scale = jnp.sqrt(squares + damp * (2.0 * trace + order * damp) + 1e-06) * 0.25
    inverse = 1.0 / scale
    shift = jnp.where(diagonal, damp * inverse, 0.0)
    for k in both:
        upper, corner = stats[k]
        fill_current_and_factor(
            slot(k, current0),
            slot(k, factor0),
            upper[:, :half] * inverse + shift,
            upper[:, half:] * inverse,
            corner * inverse + shift,
            diagonal,
        )
    for now, factor, after, factor_after in (
        (current0, factor0, current1, factor1),
        (current1, factor1, None, factor2),
    ):
        for k in both:
            fill_symmetric(slot(k, square), *symmetric_product(slot(k, factor), slot(k, factor)))
        for k in both:
            fill_symmetric(slot(k, fourth), *symmetric_product(slot(k, square), slot(k, square)))
        if factor == factor1:
            for k in both:
                fill_symmetric(
                    slot(k, iterate), *symmetric_product(slot(k, factor0), slot(k, factor1))
                )
        for k in both:
            upper, corner = symmetric_product(slot(k, fourth), slot(k, now))
            fill_current_and_factor(
                None if after is None else slot(k, after),
                slot(k, factor_after),
                upper[:, :half],
                upper[:, half:],
                corner,
                diagonal,
            )
    power = lax.rsqrt(jnp.sqrt(scale))
    for k in (1, 0):
        upper, corner = symmetric_product(slot(k, iterate), slot(k, factor2))
        fill_symmetric(slot(k, root), upper * power, corner * power)
    for k in both:
        made = work_ref[k, root]
        held_ref[k] = jnp.where(place_ref[1 + k] != 0, made, jnp.zeros_like(made))
    half_done = product(block_ref[...], work_ref[1, root]).astype(jnp.bfloat16)
    raw = product(work_ref[0, root], half_done)
    raw_ref[...] = raw
    count = order * order
    norm = jnp.sqrt(total(raw * raw) / count + 1e-06)
    graft = jnp.sqrt(trace / count + 1e-06)
    width = update_ref.shape[1]
    mine = raw_ref[:, pl.ds(pl.multiple_of(place_ref[0] * width, width), width)]
    update_ref[...] = (mine * (graft / norm)).astype(jnp.bfloat16)


def block_call(place, block, width):
    order = block.shape[0]
    return pl.pallas_call(
        block_kernel,
        out_shape=(
            jax.ShapeDtypeStruct((order, width), jnp.bfloat16),
            jax.ShapeDtypeStruct((2, order, order), jnp.bfloat16),
        ),
        in_specs=[
            pl.BlockSpec(memory_space=pltpu.SMEM),
            pl.BlockSpec(memory_space=pltpu.VMEM),
        ],
        out_specs=(
            pl.BlockSpec(memory_space=pltpu.VMEM),
            pl.BlockSpec(memory_space=pltpu.VMEM),
        ),
        scratch_shapes=[
            pltpu.VMEM((order, order), jnp.float32),
            pltpu.VMEM((2, 9, order, order), jnp.bfloat16),
        ],
        compiler_params=pltpu.CompilerParams(vmem_limit_bytes=48 * 1024 * 1024),
        cost_estimate=pl.CostEstimate(
            flops=31 * order**3, bytes_accessed=8 * order * order, transcendentals=0
        ),
        name="block_roots",
    )(place, block)


OPPOSITE = "opposite"
ROUTE = (
    (-1, (-7, -5)),
    (1, (7, 5)),
    OPPOSITE,
    (1, (3, 1)),
    (-1, (-3, -1)),
    (-2, (-6,)),
    (2, (6, 2)),
    (-2, (-2,)),
    (-4, (-4,)),
    (4, (4,)),
)


def join_kernel(sums, parity_ref, *refs):
    *operands, out_ref = refs
    rows = out_ref.shape[0] // len(sums)
    for order, terms in enumerate(sums):
        summed = None
        for operand, start, only in terms:
            value = operands[operand][pl.ds(start, rows), :].astype(jnp.float32)
            if only is not None:
                value = jnp.where(parity_ref[0] == only, value, 0.0)
            summed = value if summed is None else summed + value
        out_ref[pl.ds(order * rows, rows), :] = summed.astype(jnp.bfloat16)


def join(parity, rows, name, *sums):
    arrays, plans = [], []
    for terms in sums:
        plans.append([(len(arrays) + k, *term[1:]) for k, term in enumerate(terms)])
        arrays += [term[0] for term in terms]
    width = arrays[0].shape[1]
    vmem = pl.BlockSpec(memory_space=pltpu.VMEM)
    return pl.pallas_call(
        functools.partial(join_kernel, plans),
        out_shape=jax.ShapeDtypeStruct((len(sums) * rows, width), jnp.bfloat16),
        in_specs=[pl.BlockSpec(memory_space=pltpu.SMEM)] + [vmem] * len(arrays),
        out_specs=vmem,
        compiler_params=pltpu.CompilerParams(vmem_limit_bytes=16 * 1024 * 1024),
        cost_estimate=pl.CostEstimate(
            flops=len(arrays) * rows * width,
            bytes_accessed=2 * (len(arrays) + len(sums)) * rows * width,
            transcendentals=0,
        ),
        name=name,
    )(parity, *arrays)


def summed_piece(grads):
    size = lax.axis_size("dp")
    columns = lax.axis_size("work")
    place = lax.axis_index("dp")
    side = 1 - 2 * (lax.axis_index("work") % 2)
    pieces = grads.reshape(size, grads.shape[0] // size, grads.shape[1])
    rows = pieces.shape[1]
    parity = (place % 2)[None].astype(jnp.int32)

    def own(distance):
        return lax.dynamic_index_in_dim(pieces, (place + side * distance) % size, 0, keepdims=False)

    def moved(value, shift):
        pairs = [
            (i * columns + w, (i + (1 - 2 * (w % 2)) * shift(i)) % size * columns + w)
            for i in range(size)
            for w in range(columns)
        ]
        return lax.ppermute(value, ("dp", "work"), pairs)

    terms = {distance: [(own(distance), 0, None)] for distance in range(-7, 8)}
    for step in ROUTE:
        if step == OPPOSITE:
            arrived = moved(own(-8), lambda i: 2 if i % 2 == 0 else -2)
            terms[6].append((arrived, 0, 0))
            terms[-6].append((arrived, 0, 1))
            continue
        shift, distances = step
        leaving = [terms.pop(distance) for distance in distances]
        if all(len(parts) == 1 for parts in leaving):
            value = jnp.concatenate([parts[0][0] for parts in leaving], 0)
        else:
            value = join(parity, rows, "join_pieces", *leaving)
        arrived = moved(value, lambda i, shift=shift: shift)
        for order, distance in enumerate(distances):
            terms[distance - shift].append((arrived, order * rows, None))
    (parts,) = terms.values()
    return join(parity, rows, "join_all", parts)


def local(grads, worker_list):
    index = lax.axis_index("work")
    place = index % QUAD
    assigned = lax.dynamic_index_in_dim(worker_list[0], index // QUAD, 0, keepdims=False)
    picks = jnp.concatenate([place[None], (assigned == place).astype(jnp.int32)])
    summed = summed_piece(grads[0])
    quads = lax.axis_size("work") // QUAD
    groups = [[QUAD * q + p for p in range(QUAD)] for q in range(quads)]
    block = lax.all_gather(summed, "work", axis=1, tiled=True, axis_index_groups=groups)
    update, held = block_call(picks, block, summed.shape[1])
    return (update, held[None, None])


def solution(mesh):
    placed = (P("dp", None, "work"), P("dp", None, None))
    return jax.shard_map(
        local,
        mesh=mesh,
        in_specs=placed,
        out_specs=(P("dp", "work"), P("dp", "work", None, None, None)),
        check_vma=False,
    )
```
